128 devices in a mesh: seq: 16 (over z, x), eig: 8 (over y, core).
Axes of the slice: x: 4, y: 4, z: 4, core: 2. Of those that a mesh axis runs over, the one named last changes fastest.
Arguments:
- cand_act: bfloat16 [16, 1024, 2560], P('seq', 'eig'), may hold values from -6 to 6
- cand_grad: bfloat16 [16, 1024, 10240], P('seq', 'eig'), may hold values from -6 to 6
- query_act: bfloat16 [64, 32, 2560], P('seq'), may hold values from -6 to 6
- query_grad: bfloat16 [64, 32, 10240], P('seq', None, 'eig'), may hold values from -6 to 6
- act_basis: bfloat16 [2560, 2560], P('seq'), may hold values from -0.125 to 0.125
- grad_basis: bfloat16 [8, 1280, 1280], P('eig'), may hold values from -0.15625 to 0.15625
- eigvals: float32 [10240, 2560], P('eig'), may hold values from 0.25 to 4
- query_lists: int32 [16, 16], replicated, may hold values from 0 to 63, as said below
- valid_len: int32 [16], P('seq'), may hold values from 256 to 1024, as said below
Outputs:
- scores: float32 [16, 16], P('seq')
The draws below stay inside these ranges and needn't reach their ends.
Inputs may be any that keep to these rules, and one draw needn't show every extreme that they name: `query_lists`: each row names 16 different queries: two of the 4 queries q with q // 4 = s, for each of 8 different s. `valid_len`: at least one sequence is valid in full.
All inputs are finite; a program needn't handle non-finite values.
Results may differ from the reference program's by a relative error of at most 0.0055.
Values may be sent and summed in bfloat16 or wider, within the bound.
A program may use at most 128 MiB of HBM per device.

```python
import math
import jax
import jax.numpy as jnp
from jax import lax

DW = 2560
FW = 10240
NBLK = 8
GB = 1280
LEN = 1024
Q_DEV = 4
LQ = 32
KQ = 16
CANDS = 16
QUERIES = 64


def draw_query_lists(key, part):
    key = jax.random.fold_in(key, 11)
    subkeys = jax.random.split(key, CANDS)

    def per_candidate(subkey):
        key_owner, key_first, key_second, key_order = jax.random.split(subkey, 4)
        owners = jax.random.permutation(key_owner, QUERIES // Q_DEV)[:KQ // 2]
        first_local = jax.random.randint(key_first, (KQ // 2,), 0, Q_DEV)
        second = (first_local + 1 + jax.random.randint(key_second, (KQ // 2,), 0, Q_DEV - 1)) % Q_DEV
        picked = jnp.concatenate([owners * Q_DEV + first_local, owners * Q_DEV + second])
        return picked[jax.random.permutation(key_order, KQ)]
    return jax.vmap(per_candidate)(subkeys).astype(jnp.int32)


def draw_valid_len(key, part):
    key = jax.random.fold_in(key, 12)
    key_len, key_full = jax.random.split(key)
    lengths = jax.random.randint(key_len, (CANDS,), LEN // 4, LEN + 1)
    full_index = jax.random.randint(key_full, (), 0, CANDS)
    lengths = jnp.where(jnp.arange(CANDS) == full_index, LEN, lengths)
    return lengths.astype(jnp.int32)


def steps_of(rng, extent, cuts, smallest, high):
    loudness = 1.0
    for axis_at, blocks in cuts:
        heights = jax.random.uniform(jax.random.fold_in(jax.random.fold_in(rng, 6), axis_at), (blocks,), jnp.float32, smallest / len(cuts), high / len(cuts))
        loudness = loudness * jnp.repeat(jnp.exp(heights), extent[axis_at] // blocks).reshape((-1,) + (1,) * (len(extent) - 1 - axis_at))
    return loudness


def scatter_about(stream_key, dims, spread, limit, cuts=(), kind=jnp.bfloat16):
    level = steps_of(stream_key, dims, cuts, -0.22, 0.18) if cuts else 1.0
    array = jax.random.normal(stream_key, dims, jnp.float32) * spread * level
    return jnp.minimum(jnp.maximum(array, -limit), limit).astype(kind)


def setup_inputs(seed: int = 0) -> dict:
    seeds = jax.random.split(jax.random.key(seed), 10)
    cand_act = scatter_about(seeds[0], (CANDS, LEN, DW), 1.0, 6.0, ((0, 16), (1, 8)))
    cand_grad = scatter_about(seeds[1], (CANDS, LEN, FW), 1.0, 6.0, ((0, 16), (1, 8)))
    query_act = scatter_about(seeds[2], (QUERIES, LQ, DW), 1.0, 6.0, ((0, 16),))
    query_grad = scatter_about(seeds[3], (QUERIES, LQ, FW), 1.0, 6.0, ((0, 16), (2, 8)))
    act_basis = scatter_about(seeds[4], (DW, DW), DW ** -0.5, 0.125, ((0, 16),))
    grad_basis = scatter_about(seeds[5], (NBLK, GB, GB), GB ** -0.5, 0.15625, ((0, 8),))
    eigvals = jnp.clip(jnp.exp(math.log(4.0) - 2.7725887 * jax.random.uniform(seeds[6], (FW, DW), jnp.float32) ** steps_of(seeds[6], (FW, DW), ((0, 8),), -0.2, 0.2)), 0.25, 4.0)
    query_lists = draw_query_lists(jax.random.fold_in(seeds[9], 71), 0)
    valid_len = draw_valid_len(jax.random.fold_in(seeds[9], 71), 0)
    return dict(cand_act=cand_act, cand_grad=cand_grad, query_act=query_act, query_grad=query_grad, act_basis=act_basis, grad_basis=grad_basis, eigvals=eigvals, query_lists=query_lists, valid_len=valid_len)


def rotate_grad(grad_rows, grad_basis):
    shape_in = grad_rows.shape
    blocks = grad_rows.reshape((-1, NBLK, GB)).astype(jnp.float32)
    rotated = jnp.einsum('rbi,bij->rbj', blocks, grad_basis.astype(jnp.float32))
    return rotated.reshape(shape_in).astype(jnp.bfloat16)

def reference(cand_act, cand_grad, query_act, query_grad, act_basis, grad_basis, eigvals, query_lists, valid_len):
    rot_query_act = jnp.dot(query_act.reshape((-1, DW)), act_basis, preferred_element_type=jnp.float32)
    rot_query_act = rot_query_act.astype(jnp.bfloat16).reshape((QUERIES, LQ, DW))
    rot_query_grad = rotate_grad(query_grad, grad_basis)
    factor = 1.0 / math.sqrt(FW * DW * LEN * LQ)

    def per_candidate(inputs):
        act_rows, grad_rows, length, picked = inputs
        rot_act = jnp.dot(act_rows, act_basis, preferred_element_type=jnp.float32).astype(jnp.bfloat16)
        keep_rows = (jnp.arange(LEN, dtype=jnp.int32) < length).astype(jnp.bfloat16)
        masked_act = rot_act * keep_rows[:, None]
        rot_grad = rotate_grad(grad_rows, grad_basis)
        cross_block = jnp.dot(rot_grad.T, masked_act, preferred_element_type=jnp.float32)
        scaled = (cross_block / eigvals).astype(jnp.bfloat16)
        chosen_act = jnp.take(rot_query_act, picked, axis=0).astype(jnp.float32)
        chosen_grad = jnp.take(rot_query_grad, picked, axis=0).astype(jnp.float32)
        projected = jnp.einsum('ktj,ij->kti', chosen_act, scaled.astype(jnp.float32))
        return lax.optimization_barrier(jnp.sum(projected * chosen_grad, axis=(1, 2))) * factor
    return lax.map(per_candidate, (cand_act, cand_grad, valid_len, query_lists))
```

```python
import functools
import math

import jax
import jax.numpy as jnp
from jax import lax
from jax.experimental import pallas as pl
from jax.experimental.pallas import tpu as pltpu
from jax.sharding import PartitionSpec as P

DW = 2560
FW = 10240
LEN = 1024
LQ = 32
KQ = 16
GB = 1280
HALF = 1280
BF = jnp.bfloat16
F32 = jnp.float32
MESH = pl.DeviceIdType.MESH
FACTOR = 1.0 / math.sqrt(FW * DW * LEN * LQ)
CUTS = ((0, 768), (768, 512))
LANES = (0, -1, 1, 2)


def wrap(i):
    return lax.rem(i + 8, 4)


def mm(a, b, dims=((1,), (0,))):
    return lax.dot_general(a, b, (dims, ((), ())), preferred_element_type=F32)


def kernel(
    lists, lens, cand_act, cand_grad, query_act, query_grad, act_basis, grad_basis, eigvals,
    out,
    basis, rows, act, grads, rot_t, gbasis, recip, scaled, all_grad, slim, chosen, proj,
    raw_act, raw_grad, part,
    loc, bs, br, gs, gr, cs, cr, as_, ar, qs, qr, hs, hr, ts, tr, ps, pr,
):
    s = lax.axis_index("seq")
    e = lax.axis_index("eig")
    z, x = lax.div(s, 4), lax.rem(s, 4)
    y, h = lax.div(e, 2), lax.rem(e, 2)

    def slot(da, db):
        return 4 * wrap(z + h * da + (1 - h) * db) + wrap(x + (1 - h) * da + h * db)

    def on_seq(da, db):
        return {"seq": slot(da, db), "eig": e}

    def on_y(d):
        return {"seq": s, "eig": 2 * wrap(y + d) + h}

    def on_eig(d):
        return {"seq": s, "eig": lax.rem(e + d, 8)}

    sibling = {"seq": s, "eig": 2 * y + 1 - h}

    def remote(src, dst, send, recv, device):
        copy = pltpu.make_async_remote_copy(
            src_ref=src, dst_ref=dst, send_sem=send, recv_sem=recv,
            device_id=device, device_id_type=MESH,
        )
        copy.start()
        sent.append(copy)
        return copy

    sent = []

    my_cols = pl.ds(pl.multiple_of(h * HALF, 128), HALF)
    my_rows = pl.ds(pl.multiple_of(h * 128, 128), 128)
    local = [
        pltpu.make_async_copy(act_basis.at[:, my_cols], basis.at[s], loc.at[0]),
        pltpu.make_async_copy(query_act, raw_act, loc.at[1]),
        pltpu.make_async_copy(query_grad, raw_grad, loc.at[2]),
        pltpu.make_async_copy(grad_basis.at[0], gbasis, loc.at[3]),
        pltpu.make_async_copy(cand_act.at[0], rows.at[my_rows], loc.at[4]),
        pltpu.make_async_copy(
            cand_grad.at[0, :, pl.ds(pl.multiple_of(e * GB, 128), GB)], grads.at[e], loc.at[5]
        ),
        pltpu.make_async_copy(eigvals, recip, loc.at[6]),
    ]
    for copy in local:
        copy.start()

    barrier = pltpu.get_barrier_semaphore()
    greeted = [on_seq(1, 0), on_seq(-1, 0), on_seq(0, 1), on_seq(0, -1)]
    greeted += [on_eig(d) for d in range(1, 8)]
    for device in greeted:
        pl.semaphore_signal(barrier, inc=1, device_id=device, device_id_type=MESH)
    pl.semaphore_wait(barrier, len(greeted))

    def torus(view, own, send, recv):
        def ship(n, src, where, part, device):
            return remote(src, view(where, part), send.at[n], recv.at[n], device)

        ring = {}
        ring[0] = ship(0, own, s, None, on_seq(1, 0))
        ring[1] = ship(1, own, s, None, on_seq(-1, 0))
        for side, db in ((0, 1), (1, -1)):
            ring[4 + side] = ship(4 + side, own, s, None, on_seq(0, db))
        yield

        def second(lane):
            da = LANES[lane]
            where = slot(da, 0)
            for side, db in ((0, 1), (1, -1)):
                n = 4 + 4 * lane + side
                ring[n] = ship(n, view(where, None), where, None, on_seq(0, db))

        def onward(lane):
            da = LANES[lane]
            for side, db in ((0, 1), (1, -1)):
                ring[4 + 4 * lane + side].wait_recv()
                where = slot(da, -db)
                n = 6 + 4 * lane + side
                ring[n] = ship(n, view(where, side), where, side, on_seq(0, db))

        for side, da in ((0, 1), (1, -1)):
            ring[side].wait_recv()
            where = slot(-da, 0)
            ring[2 + side] = ship(2 + side, view(where, side), where, side, on_seq(da, 0))
            second(1 + side)
            yield
        onward(0)
        yield
        ring[2].wait_recv()
        ring[3].wait_recv()
        second(3)
        yield
        onward(1)
        yield
        onward(2)
        yield
        onward(3)
        yield
        for lane in range(4):
            ring[6 + 4 * lane].wait_recv()
            ring[7 + 4 * lane].wait_recv()
        yield

    def along_y(view, send, recv):
        def ship(n, half, where, part, device):
            ref = view(half, where, part)
            return remote(ref, ref, send.at[n], recv.at[n], device)

        got = [
            ship(0, h, y, None, on_y(1)),
            ship(1, h, y, None, on_y(-1)),
        ]
        across = [ship(4, h, y, None, sibling)]
        yield
        for side, d in ((0, 1), (1, -1)):
            got[side].wait_recv()
            where = wrap(y - d)
            got.append(ship(2 + side, h, where, side, on_y(d)))
            across.append(ship(5 + side, h, where, None, sibling))
        yield
        got[2].wait_recv()
        got[3].wait_recv()
        across.append(ship(7, h, wrap(y + 2), None, sibling))
        yield
        for copy in across:
            copy.wait_recv()
        yield

    def basis_view(where, part):
        return basis.at[where] if part is None else basis.at[where, pl.ds(80 * part, 80)]

    basis_run = torus(basis_view, act_basis.at[:, my_cols], bs, br)
    next(basis_run)

    rows_in = remote(cand_act.at[0], rows.at[my_rows], cs.at[0], cr.at[0], sibling)
    grads_in = []
    for d in (1, 7, 2, 6, 3, 5, 4):
        to = lax.rem(e + d, 8)
        cols = pl.ds(pl.multiple_of(to * GB, 128), GB)
        grads_in.append(
            remote(cand_grad.at[0, :, cols], grads.at[e], gs.at[d], gr.at[d], on_eig(d))
        )

    local[1].wait()
    r = lax.broadcasted_iota(jnp.int32, (32, 128), 0)
    c = lax.broadcasted_iota(jnp.int32, (32, 128), 1)
    want = lax.div(r, 8) * 32 + 8 * y + lax.rem(r, 8)
    pick = jnp.where(c == want, 1.0, 0.0).astype(BF)
    rows[256:288, :] = mm(pick, raw_act[...].reshape(128, DW)).astype(BF)

    local[2].wait()
    local[3].wait()
    own_grad = pl.ds(4 * s, 4)
    all_grad[own_grad] = (
        mm(raw_grad[...].reshape(128, GB), gbasis[...]).astype(BF).reshape(4, LQ, GB)
    )
    local[0].wait()
    local[6].wait()

    def invert(first, count):
        def body(i, carry):
            at = pl.ds(pl.multiple_of(i * 64, 64), 64)
            recip[at, :] = 1.0 / recip[at, :]
            return carry

        lax.fori_loop(first, first + count, body, 0)

    invert(0, 7)
    next(basis_run)
    next(basis_run)
    next(basis_run)
    invert(7, 7)
    next(basis_run)
    invert(14, 6)
    next(basis_run)
    next(basis_run)
    next(basis_run)

    local[5].wait()
    for copy in grads_in:
        copy.wait_recv()

    def rotate_grads(i, carry):
        block = grads[pl.ds(2 * i, 2)].reshape(256, GB)
        turned = mm(block, gbasis[...]).astype(BF)
        rot_t[:, pl.ds(pl.multiple_of(i * 256, 256), 256)] = turned.T
        return carry

    lax.fori_loop(0, 4, rotate_grads, 0)

    next(basis_run)

    local[4].wait()
    rows_in.wait_recv()
    length = lens[0]
    token = 256 * y + lax.broadcasted_iota(jnp.int32, (256, 1), 0)
    mine = pl.ds(pl.multiple_of(256 * y, 256), 256)
    act_runs = []

    def act_view(first, width, half, where, part):
        if part is None:
            at = pl.ds(pl.multiple_of(256 * where, 256), 256)
        else:
            at = pl.ds(pl.multiple_of(256 * where + 128 * part, 128), 128)
        return act.at[half, at, pl.ds(first, width)]

    for n, (first, width) in enumerate(CUTS):
        cols = pl.ds(first, width)
        turned = mm(rows[...], basis[:, :, cols].reshape(DW, width)).astype(BF)
        act[h, mine, cols] = jnp.where(token < length, turned[:256], jnp.zeros((), BF))
        slim[s, :, cols] = turned[256:]
        run = along_y(functools.partial(act_view, first, width), as_.at[n], ar.at[n])
        next(run)
        act_runs.append(run)

    def slim_view(where, part):
        return slim.at[where] if part is None else slim.at[where, pl.ds(16 * part, 16)]

    def grad_view(where, part):
        if part is None:
            return all_grad.at[pl.ds(4 * where, 4)]
        return all_grad.at[pl.ds(4 * where + 2 * part, 2)]

    slim_run = torus(slim_view, slim.at[s], qs, qr)
    next(slim_run)
    grad_run = torus(grad_view, grad_view(s, None), hs, hr)
    next(grad_run)
    for _ in range(8):
        next(slim_run)

    c = lax.broadcasted_iota(jnp.int32, (8, 512), 1)
    r = lax.broadcasted_iota(jnp.int32, (8, 512), 0)
    pick = jnp.concatenate(
        [jnp.where(c == lists[s, k] * 8 + r, 1.0, 0.0) for k in range(KQ)], axis=0
    ).astype(BF)
    chosen[h, y] = mm(pick, slim[...].reshape(512, HALF)).astype(BF)

    def chosen_view(half, where, part):
        if part is None:
            return chosen.at[half, where]
        return chosen.at[half, where, pl.ds(64 * part, 64)]

    chosen_run = along_y(chosen_view, ts, tr)
    next(chosen_run)

    def cross(half, first, count):
        def body(i, carry):
            cols = pl.ds(pl.multiple_of(i * 256, 256), 256)
            wide = pl.ds(pl.multiple_of(half * HALF + i * 256, 256), 256)
            block = mm(rot_t[...], act[half, :, cols])
            scaled[:, wide] = (block * recip[:, wide]).astype(BF)
            return carry

        lax.fori_loop(first, first + count, body, 0)

    next(grad_run)
    next(grad_run)
    next(act_runs[0])
    next(grad_run)
    next(grad_run)
    next(act_runs[0])
    next(act_runs[1])
    next(grad_run)
    next(act_runs[0])
    cross(0, 0, 3)
    next(chosen_run)
    next(grad_run)
    next(act_runs[1])
    next(grad_run)
    cross(1, 0, 3)
    next(chosen_run)
    next(act_runs[1])
    cross(0, 3, 2)
    cross(1, 3, 2)
    next(chosen_run)

    def project(i, carry):
        at = pl.ds(pl.multiple_of(i * 256, 256), 256)
        total = mm(chosen[0].reshape(512, HALF), scaled[at, :HALF], ((1,), (1,)))
        total += mm(chosen[1].reshape(512, HALF), scaled[at, HALF:], ((1,), (1,)))
        proj[:, :, at] = total.reshape(4, 128, 256)
        return carry

    lax.fori_loop(0, 5, project, 0)
    next(grad_run)

    def score(k, carry):
        grad = all_grad[lists[s, k]].astype(F32)
        at = pl.ds(pl.multiple_of(8 * k, 8), 8)
        total = proj[0, at] * grad[0:8]
        for n in range(1, 4):
            total += proj[n, at] * grad[8 * n : 8 * n + 8]
        folded = total[:, :128]
        for n in range(1, GB // 128):
            folded += total[:, 128 * n : 128 * n + 128]
        part[e, pl.ds(k, 1), :] = jnp.sum(folded, axis=0, keepdims=True)
        return carry

    lax.fori_loop(0, KQ, score, 0)

    parts_in = [
        remote(part.at[e], part.at[e], ps.at[d], pr.at[d], on_eig(d))
        for d in range(1, 8)
    ]
    for copy in parts_in:
        copy.wait_recv()
    full = part[0]
    for block in range(1, 8):
        full += part[block]
    full = jnp.concatenate([full, jnp.zeros((128 - KQ, 128), F32)], axis=0)
    out[...] = (jnp.sum(full.T, axis=0, keepdims=True) * FACTOR)[:, :KQ]

    for copy in sent:
        copy.wait_send()


def shards(
    cand_act, cand_grad, query_act, query_grad, act_basis, grad_basis, eigvals, query_lists,
    valid_len,
):
    anywhere = pl.BlockSpec(memory_space=pl.ANY)
    scalars = pl.BlockSpec(memory_space=pltpu.SMEM)
    dma = pltpu.SemaphoreType.DMA
    return pl.pallas_call(
        kernel,
        out_shape=jax.ShapeDtypeStruct((1, KQ), F32),
        in_specs=[scalars, scalars] + [anywhere] * 7,
        out_specs=pl.BlockSpec(memory_space=pltpu.VMEM),
        scratch_shapes=[
            pltpu.VMEM((16, 160, HALF), BF),
            pltpu.VMEM((288, DW), BF),
            pltpu.VMEM((2, LEN, HALF), BF),
            pltpu.VMEM((8, 128, GB), BF),
            pltpu.VMEM((GB, LEN), BF),
            pltpu.VMEM((GB, GB), BF),
            pltpu.VMEM((GB, DW), F32),
            pltpu.VMEM((GB, DW), BF),
            pltpu.VMEM((64, LQ, GB), BF),
            pltpu.VMEM((16, 32, HALF), BF),
            pltpu.VMEM((2, 4, 128, HALF), BF),
            pltpu.VMEM((4, 128, GB), F32),
            pltpu.VMEM((4, LQ, DW), BF),
            pltpu.VMEM((4, LQ, GB), BF),
            pltpu.VMEM((8, KQ, 128), F32),
            dma((7,)),
            dma((20,)), dma((20,)),
            dma((8,)), dma((8,)),
            dma((1,)), dma((1,)),
            dma((2, 8)), dma((2, 8)),
            dma((20,)), dma((20,)),
            dma((20,)), dma((20,)),
            dma((8,)), dma((8,)),
            dma((8,)), dma((8,)),
        ],
        compiler_params=pltpu.CompilerParams(
            collective_id=0, has_side_effects=True, vmem_limit_bytes=63 * 2**20
        ),
        name="influence",
    )(
        query_lists, valid_len, cand_act, cand_grad, query_act, query_grad, act_basis,
        grad_basis, eigvals,
    )


def solution(mesh):
    placed = (
        P("seq", "eig", None),
        P("seq", "eig", None),
        P("seq", None, None),
        P("seq", None, "eig"),
        P("seq", None),
        P("eig", None, None),
        P("eig", None),
        P(),
        P("seq"),
    )
    return jax.shard_map(
        shards, mesh=mesh, in_specs=placed, out_specs=P("seq", None), check_vma=False
    )
```

```python
import functools
import math

import jax
import jax.numpy as jnp
from jax import lax
from jax.experimental import pallas as pl
from jax.experimental.pallas import tpu as pltpu
from jax.sharding import PartitionSpec as P

DW = 2560
FW = 10240
LEN = 1024
LQ = 32
KQ = 16
GB = 1280
HALF = 1280
QUARTER = 640
BF = jnp.bfloat16
F32 = jnp.float32
MESH = pl.DeviceIdType.MESH
FACTOR = 1.0 / math.sqrt(FW * DW * LEN * LQ)
ORDER = (
    "brGwbbbbirGbbbib",
    "gMasigissssssagsgskgtg",
    "tatgaXgaxxkaqaXpg",
)
LANES = (0, -1, 1, 2)


def wrap(i):
    return lax.rem(i + 8, 4)


def mm(a, b, dims=((1,), (0,))):
    return lax.dot_general(a, b, (dims, ((), ())), preferred_element_type=F32)


def kernel(
    lists, lens, cand_act, cand_grad, query_act, query_grad, act_basis, grad_basis, eigvals,
    out,
    basis, rows, total, act, grads, rot_t, gbasis, recip, scaled, all_grad, slim, chosen, proj, begun,
    raw_grad, part,
    loc, bs, br, gs, gr, cs, cr, as_, ar, qs, qr, hs, hr, ts, tr, ps, pr,
):
    s = lax.axis_index("seq")
    e = lax.axis_index("eig")
    z, x = lax.div(s, 4), lax.rem(s, 4)
    y, h = lax.div(e, 2), lax.rem(e, 2)
    parity = lax.rem(y, 2)
    other = 1 - parity
    lower = 1 - lax.rem(y + h, 2)

    def slot(da, db):
        return 4 * wrap(z + h * da + (1 - h) * db) + wrap(x + (1 - h) * da + h * db)

    def on_seq(da, db):
        return {"seq": slot(da, db), "eig": e}

    def on_y(d):
        return {"seq": s, "eig": 2 * wrap(y + d) + h}

    def on_eig(d):
        return {"seq": s, "eig": lax.rem(e + d, 8)}

    sibling = {"seq": s, "eig": 2 * y + 1 - h}

    def remote(src, dst, send, recv, device):
        copy = pltpu.make_async_remote_copy(
            src_ref=src, dst_ref=dst, send_sem=send, recv_sem=recv,
            device_id=device, device_id_type=MESH,
        )
        copy.start()
        sent.append(copy)
        return copy

    sent = []

    def at_rows(i):
        return pl.ds(pl.multiple_of(128 * i, 128), 128)

    quarter = pl.ds(pl.multiple_of(parity * HALF + h * QUARTER, 128), QUARTER)
    block_rows = pl.ds(pl.multiple_of(160 * s, 32), 160)
    place = 2 * wrap(y - 1 + lower) + 1 - lower
    local = [
        pltpu.make_async_copy(act_basis.at[:, quarter], basis.at[block_rows], loc.at[0]),
        pltpu.make_async_copy(query_grad, raw_grad, loc.at[1]),
        pltpu.make_async_copy(grad_basis.at[0], gbasis, loc.at[2]),
        pltpu.make_async_copy(cand_act.at[0], rows.at[at_rows(1 + lower)], loc.at[3]),
        pltpu.make_async_copy(
            cand_grad.at[0, :, pl.ds(pl.multiple_of(e * GB, 128), GB)], grads.at[place], loc.at[4]
        ),
        pltpu.make_async_copy(eigvals, recip, loc.at[5]),
    ]
    local += [
        pltpu.make_async_copy(query_act.at[n], rows.at[pl.ds(512 + LQ * n, LQ)], loc.at[6 + n])
        for n in range(4)
    ]

    barrier = pltpu.get_barrier_semaphore()
    greeted = [on_seq(1, 0), on_seq(-1, 0), on_seq(0, 1), on_seq(0, -1)]
    greeted += [on_eig(d) for d in range(1, 8)]
    for device in greeted:
        pl.semaphore_signal(barrier, inc=1, device_id=device, device_id_type=MESH)
    pl.semaphore_wait(barrier, len(greeted))

    def torus(view_of, own_of, send, recv, width=QUARTER):
        cols = pl.ds(0, width)
        view = functools.partial(view_of, cols)
        own = own_of(cols)

        def ship(n, src, where, part, device):
            return remote(src, view(where, part), send.at[n], recv.at[n], device)

        ring = {}
        ring[0] = ship(0, own, s, None, on_seq(1, 0))
        ring[1] = ship(1, own, s, None, on_seq(-1, 0))
        for side, db in ((0, 1), (1, -1)):
            ring[4 + side] = ship(4 + side, own, s, None, on_seq(0, db))
        yield

        def second(lane):
            da = LANES[lane]
            where = slot(da, 0)
            for side, db in ((0, 1), (1, -1)):
                n = 4 + 4 * lane + side
                ring[n] = ship(n, view(where, None), where, None, on_seq(0, db))

        def onward(lane):
            da = LANES[lane]
            for side, db in ((0, 1), (1, -1)):
                ring[4 + 4 * lane + side].wait_recv()
                where = slot(da, -db)
                n = 6 + 4 * lane + side
                ring[n] = ship(n, view(where, side), where, side, on_seq(0, db))

        for side, da in ((0, 1), (1, -1)):
            ring[side].wait_recv()
            where = slot(-da, 0)
            ring[2 + side] = ship(2 + side, view(where, side), where, side, on_seq(da, 0))
            second(1 + side)
            yield
        ring[2].wait_recv()
        ring[3].wait_recv()
        second(3)
        yield
        for lane in range(4):
            onward(lane)
            yield
        for lane in range(4):
            ring[6 + 4 * lane].wait_recv()
            ring[7 + 4 * lane].wait_recv()
        yield

    def basis_view(cols, where, part):
        if part is None:
            return basis.at[pl.ds(pl.multiple_of(160 * where, 32), 160), cols]
        return basis.at[pl.ds(pl.multiple_of(160 * where + 80 * part, 16), 80), cols]

    def own_basis(cols):
        first = parity * HALF + h * QUARTER + cols.start
        return act_basis.at[:, pl.ds(pl.multiple_of(first, 128), cols.size)]

    partner = {"seq": s, "eig": 2 * wrap(y + 2 * lower - 1) + h}

    def share_rows():
        near = rows.at[at_rows(1 + lower)]
        far = rows.at[at_rows(3 * lower)]
        first = remote(
            cand_act.at[0], rows.at[at_rows(3 * (1 - lower))], cs.at[0], cr.at[0], partner
        )
        across = [remote(cand_act.at[0], near, cs.at[1], cr.at[1], sibling)]
        yield
        first.wait_recv()
        across.append(remote(far, far, cs.at[2], cr.at[2], sibling))
        yield
        local[3].wait()
        for copy in across:
            copy.wait_recv()
        yield

    def share_grads():
        grads_in = []
        for offsets in ((2, 6), (3, 5, 4, 1, 7)):
            for d in offsets:
                to = lax.rem(e + d, 8)
                cols = pl.ds(pl.multiple_of(to * GB, 128), GB)
                copy = remote(
                    cand_grad.at[0, :, cols], grads.at[place], gs.at[d], gr.at[d], on_eig(d)
                )
                grads_in.append(copy)
            yield
        local[4].wait()
        for copy in grads_in:
            copy.wait_recv()
        yield

    def rotate_grads():
        next(run["G"])

        def turn(i, carry):
            cols = pl.ds(pl.multiple_of(i * 256, 256), 256)
            turned = mm(grads[...].reshape(LEN, GB), gbasis[:, cols]).astype(BF)
            rot_t[cols, :] = turned.T
            return carry

        for first, last in ((0, 2), (2, 4), (4, 5)):
            lax.fori_loop(first, last, turn, 0)
            yield

    def own_grads():
        local[1].wait()
        local[2].wait()

        def turn(i, carry):
            cols = pl.ds(pl.multiple_of(i * 256, 256), 256)
            turned = mm(raw_grad[...].reshape(128, GB), gbasis[:, cols]).astype(BF)
            all_grad[pl.ds(4 * s, 4), :, cols] = turned.reshape(4, LQ, 256)
            return carry

        lax.fori_loop(0, 5, turn, 0)
        yield

    def grad_view(cols, where, part):
        if part is None:
            return all_grad.at[pl.ds(4 * where, 4), :, cols]
        return all_grad.at[pl.ds(4 * where + 2 * part, 2), :, cols]

    def invert():
        local[5].wait()

        def body(i, carry):
            at = pl.ds(pl.multiple_of(i * 64, 64), 64)
            recip[at, :] = 1.0 / recip[at, :]
            return carry

        for first in range(0, 20, 5):
            lax.fori_loop(first, first + 5, body, 0)
            yield

    mine = pl.ds(pl.multiple_of(h * QUARTER, 128), QUARTER)

    def rotate_rows():
        local[0].wait()
        for copy in local[6:]:
            copy.wait()
        next(run["r"])

        def add(i, carry):
            at = pl.ds(pl.multiple_of(i * 512, 512), 512)
            total[...] += mm(rows[:, at], basis[at, :])
            return carry

        total[...] = jnp.zeros_like(total)
        lax.fori_loop(0, 5, add, 0)
        length = lens[0]
        r = lax.broadcasted_iota(jnp.int32, (128, 1), 0)
        for n, (chip, core) in enumerate(((-1, other), (0, other), (0, parity), (1, parity))):
            token = 256 * wrap(y + chip) + 128 * core + r
            turned = total[128 * n : 128 * n + 128].astype(BF)
            at = pl.ds(pl.multiple_of(256 * wrap(y - 1 + n // 2) + 128 * (n % 2), 128), 128)
            act[parity, at, mine] = jnp.where(token < length, turned, jnp.zeros((), BF))
        slim[pl.ds(4 * s, 4)] = total[512:640].astype(BF).reshape(4, LQ, QUARTER)
        yield

    def act_view(half, block):
        return act.at[half, pl.ds(pl.multiple_of(256 * block, 256), 256), mine]

    def gather_act():
        def ship(n, half, block, device):
            view = act_view(half, block)
            return remote(view, view, as_.at[n], ar.at[n], device)

        ring = {}
        for side, d in ((0, 1), (1, -1)):
            ring[side] = ship(side, parity, wrap(y - 1 + side), on_y(d))
        for side, d in ((0, 1), (1, -1)):
            ring[2 + side] = ship(2 + side, parity, wrap(y - side), on_y(d))
        across = [ship(6 + side, parity, wrap(y - 1 + side), sibling) for side in (0, 1)]
        yield
        for side, d in ((0, 1), (1, -1)):
            ring[side].wait_recv()
            block = wrap(y - d - 1 + side)
            ring[4 + side] = ship(4 + side, other, block, on_y(d))
            across.append(ship(8 + side, other, block, sibling))
        yield
        for side, d in ((0, 1), (1, -1)):
            ring[2 + side].wait_recv()
            across.append(ship(10 + side, other, wrap(y - d - side), sibling))
        yield
        for copy in across[:2]:
            copy.wait_recv()
        yield
        for copy in across[2:6]:
            copy.wait_recv()
        yield
        for side in (0, 1):
            ring[4 + side].wait_recv()
            across.append(ship(12 + side, parity, wrap(y + 1 + side), sibling))
        yield
        for copy in across[6:]:
            copy.wait_recv()
        yield

    def slim_view(cols, where, part):
        if part is None:
            return slim.at[pl.ds(4 * where, 4), :, cols]
        return slim.at[pl.ds(4 * where + 2 * part, 2), :, cols]

    def choose():
        def ship(n, half, piece, device):
            view = chosen.at[half, :, mine]
            if piece is not None:
                view = chosen.at[half, pl.ds(256 * piece, 256), mine]
            return remote(view, view, ts.at[n], tr.at[n], device)

        for k in range(KQ):
            chosen[parity, LQ * k : LQ * k + LQ, mine] = slim[lists[s, k]]
        near = [ship(0, parity, 0, on_y(1)), ship(1, parity, 1, on_y(-1))]
        across = [ship(2, parity, None, sibling)]
        yield
        for side in (0, 1):
            near[side].wait_recv()
            across.append(ship(3 + side, other, side, sibling))
        yield
        for copy in across[1:]:
            copy.wait_recv()
        yield
        across[0].wait_recv()
        yield

    def cross_other():
        def body(i, carry):
            cols = pl.ds(pl.multiple_of(i * 256, 256), 256)
            wide = pl.ds(pl.multiple_of(other * HALF + i * 256, 256), 256)
            block = mm(rot_t[...], act[other, :, cols])
            scaled[other, :, cols] = (block * recip[:, wide]).astype(BF)
            return carry

        for first, last in ((0, 2), (2, 5)):
            lax.fori_loop(first, last, body, 0)
            yield

    def cross_own():
        def two(block, cols):
            at = [pl.ds(pl.multiple_of(256 * wrap(block + n), 256), 256) for n in (0, 1)]
            return mm(rot_t[:, at[0]], act[parity, at[0], cols]) + mm(
                rot_t[:, at[1]], act[parity, at[1], cols]
            )

        def begin(i, carry):
            cols = pl.ds(pl.multiple_of(i * 256, 256), 256)
            begun[:, cols] = two(y - 1, cols)
            return carry

        def finish(i, carry):
            cols = pl.ds(pl.multiple_of(i * 256, 256), 256)
            wide = pl.ds(pl.multiple_of(parity * HALF + i * 256, 256), 256)
            block = begun[:, cols] + two(y + 1, cols)
            scaled[parity, :, cols] = (block * recip[:, wide]).astype(BF)
            return carry

        lax.fori_loop(0, 5, begin, 0)
        yield
        lax.fori_loop(0, 5, finish, 0)
        yield

    def project(half, add):
        next(run["k"])
        block = mm(chosen[half], scaled[half], ((1,), (1,)))
        proj[...] = proj[...] + block if add else block
        yield

    run = {
        "b": torus(basis_view, own_basis, bs, br),
        "r": share_rows(),
        "G": share_grads(),
        "w": own_grads(),
        "g": torus(grad_view, lambda cols: grad_view(cols, s, None), hs, hr, GB),
        "s": torus(slim_view, lambda cols: slim_view(cols, s, None), qs, qr),
        "i": invert(),
        "M": rotate_rows(),
        "a": gather_act(),
        "t": rotate_grads(),
        "k": choose(),
        "x": cross_other(),
        "X": cross_own(),
        "p": project(parity, True),
        "q": project(other, False),
    }
    order = "".join(ORDER)
    for n, letter in enumerate(order):
        if n == 2:
            for copy in local:
                copy.start()
        next(run[letter])
    for stages in run.values():
        assert next(stages, 0) == 0

    def score(k, carry):
        grad = all_grad[lists[s, k]].astype(F32)
        at = pl.ds(pl.multiple_of(LQ * k, LQ), LQ)
        folded = proj[at, :128] * grad[:, :128]
        for n in range(1, GB // 128):
            cols = slice(128 * n, 128 * n + 128)
            folded += proj[at, cols] * grad[:, cols]
        part[e, pl.ds(k, 1), :] = jnp.sum(folded, axis=0, keepdims=True)
        return carry

    lax.fori_loop(0, KQ, score, 0)

    parts_in = [
        remote(part.at[e], part.at[e], ps.at[d], pr.at[d], on_eig(d))
        for d in range(1, 8)
    ]
    for copy in parts_in:
        copy.wait_recv()
    full = part[0]
    for block in range(1, 8):
        full += part[block]
    full = jnp.concatenate([full, jnp.zeros((128 - KQ, 128), F32)], axis=0)
    out[...] = (jnp.sum(full.T, axis=0, keepdims=True) * FACTOR)[:, :KQ]

    for copy in sent:
        copy.wait_send()


def shards(
    cand_act, cand_grad, query_act, query_grad, act_basis, grad_basis, eigvals, query_lists,
    valid_len,
):
    anywhere = pl.BlockSpec(memory_space=pl.ANY)
    scalars = pl.BlockSpec(memory_space=pltpu.SMEM)
    dma = pltpu.SemaphoreType.DMA
    return pl.pallas_call(
        kernel,
        out_shape=jax.ShapeDtypeStruct((1, KQ), F32),
        in_specs=[scalars, scalars] + [anywhere] * 7,
        out_specs=pl.BlockSpec(memory_space=pltpu.VMEM),
        scratch_shapes=[
            pltpu.VMEM((DW, QUARTER), BF),
            pltpu.VMEM((640, DW), BF),
            pltpu.VMEM((640, QUARTER), F32),
            pltpu.VMEM((2, LEN, HALF), BF),
            pltpu.VMEM((8, 128, GB), BF),
            pltpu.VMEM((GB, LEN), BF),
            pltpu.VMEM((GB, GB), BF),
            pltpu.VMEM((GB, DW), F32),
            pltpu.VMEM((2, GB, HALF), BF),
            pltpu.VMEM((64, LQ, GB), BF),
            pltpu.VMEM((64, LQ, QUARTER), BF),
            pltpu.VMEM((2, KQ * LQ, HALF), BF),
            pltpu.VMEM((KQ * LQ, GB), F32),
            pltpu.VMEM((GB, HALF), F32),
            pltpu.VMEM((4, LQ, GB), BF),
            pltpu.VMEM((8, KQ, 128), F32),
            dma((10,)),
            dma((20,)), dma((20,)),
            dma((8,)), dma((8,)),
            dma((3,)), dma((3,)),
            dma((14,)), dma((14,)),
            dma((20,)), dma((20,)),
            dma((20,)), dma((20,)),
            dma((5,)), dma((5,)),
            dma((8,)), dma((8,)),
        ],
        compiler_params=pltpu.CompilerParams(
            collective_id=0, has_side_effects=True, vmem_limit_bytes=63 * 2**20
        ),
        name="influence",
    )(
        query_lists, valid_len, cand_act, cand_grad, query_act, query_grad, act_basis,
        grad_basis, eigvals,
    )


def solution(mesh):
    placed = (
        P("seq", "eig", None),
        P("seq", "eig", None),
        P("seq", None, None),
        P("seq", None, "eig"),
        P("seq", None),
        P("eig", None, None),
        P("eig", None),
        P(),
        P("seq"),
    )
    return jax.shard_map(
        shards, mesh=mesh, in_specs=placed, out_specs=P("seq", None), check_vma=False
    )
```

```python
import functools
import math

import jax
import jax.numpy as jnp
from jax import lax
from jax.experimental import pallas as pl
from jax.experimental.pallas import tpu as pltpu
from jax.sharding import PartitionSpec as P

DW = 2560
FW = 10240
LEN = 1024
LQ = 32
KQ = 16
GB = 1280
HALF = 1280
QUARTER = 640
BF = jnp.bfloat16
F32 = jnp.float32
MESH = pl.DeviceIdType.MESH
FACTOR = 1.0 / math.sqrt(FW * DW * LEN * LQ)
ORDER = (
    "brGwbbbbirGbbbib",
    "gMsigissasssatagtssgskggta",
    "XgaxaxgakXkpkpg",
)
LANES = (0, -1, 1, 2)


def wrap(i):
    return lax.rem(i + 8, 4)


def mm(a, b, dims=((1,), (0,))):
    return lax.dot_general(a, b, (dims, ((), ())), preferred_element_type=F32)


def kernel(
    lists, lens, cand_act, cand_grad, query_act, query_grad, act_basis, grad_basis, eigvals,
    out,
    basis, rows, total, act, grads, rot_t, gbasis, recip, scaled, all_grad, slim, chosen, proj, begun,
    raw_grad, part,
    loc, bs, br, gs, gr, cs, cr, as_, ar, qs, qr, hs, hr, ts, tr, ps, pr,
):
    s = lax.axis_index("seq")
    e = lax.axis_index("eig")
    z, x = lax.div(s, 4), lax.rem(s, 4)
    y, h = lax.div(e, 2), lax.rem(e, 2)
    parity = lax.rem(y, 2)
    other = 1 - parity
    lower = 1 - lax.rem(y + h, 2)

    def slot(da, db):
        return 4 * wrap(z + h * da + (1 - h) * db) + wrap(x + (1 - h) * da + h * db)

    def on_seq(da, db):
        return {"seq": slot(da, db), "eig": e}

    def on_y(d):
        return {"seq": s, "eig": 2 * wrap(y + d) + h}

    def on_eig(d):
        return {"seq": s, "eig": lax.rem(e + d, 8)}

    sibling = {"seq": s, "eig": 2 * y + 1 - h}

    def remote(src, dst, send, recv, device):
        copy = pltpu.make_async_remote_copy(
            src_ref=src, dst_ref=dst, send_sem=send, recv_sem=recv,
            device_id=device, device_id_type=MESH,
        )
        copy.start()
        sent.append(copy)
        return copy

    sent = []

    def at_rows(i):
        return pl.ds(pl.multiple_of(128 * i, 128), 128)

    quarter = pl.ds(pl.multiple_of(parity * HALF + h * QUARTER, 128), QUARTER)
    block_rows = pl.ds(pl.multiple_of(160 * s, 32), 160)
    place = 2 * wrap(y - 1 + lower) + 1 - lower
    local = [
        pltpu.make_async_copy(act_basis.at[:, quarter], basis.at[block_rows], loc.at[0]),
        pltpu.make_async_copy(query_grad, raw_grad, loc.at[1]),
        pltpu.make_async_copy(grad_basis.at[0], gbasis, loc.at[2]),
        pltpu.make_async_copy(cand_act.at[0], rows.at[at_rows(1 + lower)], loc.at[3]),
        pltpu.make_async_copy(
            cand_grad.at[0, :, pl.ds(pl.multiple_of(e * GB, 128), GB)], grads.at[place], loc.at[4]
        ),
        pltpu.make_async_copy(eigvals, recip, loc.at[5]),
    ]
    local += [
        pltpu.make_async_copy(query_act.at[n], rows.at[pl.ds(512 + LQ * n, LQ)], loc.at[6 + n])
        for n in range(4)
    ]

    barrier = pltpu.get_barrier_semaphore()
    greeted = [on_seq(1, 0), on_seq(-1, 0), on_seq(0, 1), on_seq(0, -1)]
    greeted += [on_eig(d) for d in range(1, 8)]
    for device in greeted:
        pl.semaphore_signal(barrier, inc=1, device_id=device, device_id_type=MESH)
    pl.semaphore_wait(barrier, len(greeted))

    def torus(view_of, own_of, send, recv, width=QUARTER):
        cols = pl.ds(0, width)
        view = functools.partial(view_of, cols)
        own = own_of(cols)

        def ship(n, src, where, part, device):
            return remote(src, view(where, part), send.at[n], recv.at[n], device)

        ring = {}
        ring[0] = ship(0, own, s, None, on_seq(1, 0))
        ring[1] = ship(1, own, s, None, on_seq(-1, 0))
        for side, db in ((0, 1), (1, -1)):
            ring[4 + side] = ship(4 + side, own, s, None, on_seq(0, db))
        yield

        def second(lane):
            da = LANES[lane]
            where = slot(da, 0)
            for side, db in ((0, 1), (1, -1)):
                n = 4 + 4 * lane + side
                ring[n] = ship(n, view(where, None), where, None, on_seq(0, db))

        def onward(lane):
            da = LANES[lane]
            for side, db in ((0, 1), (1, -1)):
                ring[4 + 4 * lane + side].wait_recv()
                where = slot(da, -db)
                n = 6 + 4 * lane + side
                ring[n] = ship(n, view(where, side), where, side, on_seq(0, db))

        for side, da in ((0, 1), (1, -1)):
            ring[side].wait_recv()
            where = slot(-da, 0)
            ring[2 + side] = ship(2 + side, view(where, side), where, side, on_seq(da, 0))
            second(1 + side)
            yield
        ring[2].wait_recv()
        ring[3].wait_recv()
        second(3)
        yield
        for lane in range(4):
            onward(lane)
            yield
        for lane in range(4):
            ring[6 + 4 * lane].wait_recv()
            ring[7 + 4 * lane].wait_recv()
        yield

    def basis_view(cols, where, part):
        if part is None:
            return basis.at[pl.ds(pl.multiple_of(160 * where, 32), 160), cols]
        return basis.at[pl.ds(pl.multiple_of(160 * where + 80 * part, 16), 80), cols]

    def own_basis(cols):
        first = parity * HALF + h * QUARTER + cols.start
        return act_basis.at[:, pl.ds(pl.multiple_of(first, 128), cols.size)]

    partner = {"seq": s, "eig": 2 * wrap(y + 2 * lower - 1) + h}

    def share_rows():
        near = rows.at[at_rows(1 + lower)]
        far = rows.at[at_rows(3 * lower)]
        first = remote(
            cand_act.at[0], rows.at[at_rows(3 * (1 - lower))], cs.at[0], cr.at[0], partner
        )
        across = [remote(cand_act.at[0], near, cs.at[1], cr.at[1], sibling)]
        yield
        first.wait_recv()
        across.append(remote(far, far, cs.at[2], cr.at[2], sibling))
        yield
        local[3].wait()
        for copy in across:
            copy.wait_recv()
        yield

    def share_grads():
        grads_in = []
        for offsets in ((2, 6), (3, 5, 4, 1, 7)):
            for d in offsets:
                to = lax.rem(e + d, 8)
                cols = pl.ds(pl.multiple_of(to * GB, 128), GB)
                copy = remote(
                    cand_grad.at[0, :, cols], grads.at[place], gs.at[d], gr.at[d], on_eig(d)
                )
                grads_in.append(copy)
            yield
        local[4].wait()
        for copy in grads_in:
            copy.wait_recv()
        yield

    def rotate_grads():
        next(run["G"])

        def turn(i, carry):
            cols = pl.ds(pl.multiple_of(i * 256, 256), 256)
            turned = mm(grads[...].reshape(LEN, GB), gbasis[:, cols]).astype(BF)
            rot_t[cols, :] = turned.T
            return carry

        for first, last in ((0, 2), (2, 4), (4, 5)):
            lax.fori_loop(first, last, turn, 0)
            yield

    def own_grads():
        local[1].wait()
        local[2].wait()

        def turn(i, carry):
            cols = pl.ds(pl.multiple_of(i * 256, 256), 256)
            turned = mm(raw_grad[...].reshape(128, GB), gbasis[:, cols]).astype(BF)
            all_grad[pl.ds(4 * s, 4), :, cols] = turned.reshape(4, LQ, 256)
            return carry

        lax.fori_loop(0, 5, turn, 0)
        yield

    def grad_view(cols, where, part):
        if part is None:
            return all_grad.at[pl.ds(4 * where, 4), :, cols]
        return all_grad.at[pl.ds(4 * where + 2 * part, 2), :, cols]

    def invert():
        local[5].wait()

        def body(i, carry):
            at = pl.ds(pl.multiple_of(i * 64, 64), 64)
            recip[at, :] = 1.0 / recip[at, :]
            return carry

        for first in range(0, 20, 5):
            lax.fori_loop(first, first + 5, body, 0)
            yield

    mine = pl.ds(pl.multiple_of(h * QUARTER, 128), QUARTER)

    def rotate_rows():
        local[0].wait()
        for copy in local[6:]:
            copy.wait()
        next(run["r"])

        def add(i, carry):
            at = pl.ds(pl.multiple_of(i * 512, 512), 512)
            total[...] += mm(rows[:, at], basis[at, :])
            return carry

        total[...] = jnp.zeros_like(total)
        lax.fori_loop(0, 5, add, 0)
        length = lens[0]
        r = lax.broadcasted_iota(jnp.int32, (128, 1), 0)
        for n, (chip, core) in enumerate(((-1, other), (0, other), (0, parity), (1, parity))):
            token = 256 * wrap(y + chip) + 128 * core + r
            turned = total[128 * n : 128 * n + 128].astype(BF)
            at = pl.ds(pl.multiple_of(256 * wrap(y - 1 + n // 2) + 128 * (n % 2), 128), 128)
            act[parity, at, mine] = jnp.where(token < length, turned, jnp.zeros((), BF))
        slim[pl.ds(4 * s, 4)] = total[512:640].astype(BF).reshape(4, LQ, QUARTER)
        yield

    def act_view(half, block):
        return act.at[half, pl.ds(pl.multiple_of(256 * block, 256), 256), mine]

    def gather_act():
        def ship(n, half, block, device):
            view = act_view(half, block)
            return remote(view, view, as_.at[n], ar.at[n], device)

        ring = {}
        for side, d in ((0, 1), (1, -1)):
            ring[side] = ship(side, parity, wrap(y - 1 + side), on_y(d))
        for side, d in ((0, 1), (1, -1)):
            ring[2 + side] = ship(2 + side, parity, wrap(y - side), on_y(d))
        across = [ship(6 + side, parity, wrap(y - 1 + side), sibling) for side in (0, 1)]
        yield
        for copy in across[:2]:
            copy.wait_recv()
        yield
        for side, d in ((0, 1), (1, -1)):
            ring[side].wait_recv()
            block = wrap(y - d - 1 + side)
            ring[4 + side] = ship(4 + side, other, block, on_y(d))
            across.append(ship(8 + side, other, block, sibling))
        yield
        for side, d in ((0, 1), (1, -1)):
            ring[2 + side].wait_recv()
            across.append(ship(10 + side, other, wrap(y - d - side), sibling))
        yield
        for copy in across[2:6]:
            copy.wait_recv()
        yield
        for side in (0, 1):
            ring[4 + side].wait_recv()
            across.append(ship(12 + side, parity, wrap(y + 1 + side), sibling))
        yield
        for copy in across[6:]:
            copy.wait_recv()
        yield

    def slim_view(cols, where, part):
        if part is None:
            return slim.at[pl.ds(4 * where, 4), :, cols]
        return slim.at[pl.ds(4 * where + 2 * part, 2), :, cols]

    def choose():
        def ship(n, half, piece, device):
            view = chosen.at[half, :, mine]
            if piece is not None:
                view = chosen.at[half, pl.ds(256 * piece, 256), mine]
            return remote(view, view, ts.at[n], tr.at[n], device)

        for k in range(KQ):
            chosen[parity, LQ * k : LQ * k + LQ, mine] = slim[lists[s, k]]
        near = [ship(0, parity, 0, on_y(1)), ship(1, parity, 1, on_y(-1))]
        across = [ship(2, parity, None, sibling)]
        yield
        across[0].wait_recv()
        yield
        for side in (0, 1):
            near[side].wait_recv()
            across.append(ship(3 + side, other, side, sibling))
        yield
        for copy in across[1:]:
            copy.wait_recv()
        yield

    def cross_other():
        def body(i, carry):
            cols = pl.ds(pl.multiple_of(i * 256, 256), 256)
            wide = pl.ds(pl.multiple_of(other * HALF + i * 256, 256), 256)
            block = mm(rot_t[...], act[other, :, cols])
            scaled[other, :, cols] = (block * recip[:, wide]).astype(BF)
            return carry

        for first, last in ((0, 2), (2, 5)):
            lax.fori_loop(first, last, body, 0)
            yield

    def cross_own():
        def two(block, cols):
            at = [pl.ds(pl.multiple_of(256 * wrap(block + n), 256), 256) for n in (0, 1)]
            return mm(rot_t[:, at[0]], act[parity, at[0], cols]) + mm(
                rot_t[:, at[1]], act[parity, at[1], cols]
            )

        def begin(i, carry):
            cols = pl.ds(pl.multiple_of(i * 256, 256), 256)
            begun[:, cols] = two(y - 1, cols)
            return carry

        def finish(i, carry):
            cols = pl.ds(pl.multiple_of(i * 256, 256), 256)
            wide = pl.ds(pl.multiple_of(parity * HALF + i * 256, 256), 256)
            block = begun[:, cols] + two(y + 1, cols)
            scaled[parity, :, cols] = (block * recip[:, wide]).astype(BF)
            return carry

        lax.fori_loop(0, 5, begin, 0)
        yield
        lax.fori_loop(0, 5, finish, 0)
        yield

    def project():
        proj[...] = mm(chosen[parity], scaled[parity], ((1,), (1,)))
        yield
        proj[...] += mm(chosen[other], scaled[other], ((1,), (1,)))
        yield

    run = {
        "b": torus(basis_view, own_basis, bs, br),
        "r": share_rows(),
        "G": share_grads(),
        "w": own_grads(),
        "g": torus(grad_view, lambda cols: grad_view(cols, s, None), hs, hr, GB),
        "s": torus(slim_view, lambda cols: slim_view(cols, s, None), qs, qr),
        "i": invert(),
        "M": rotate_rows(),
        "a": gather_act(),
        "t": rotate_grads(),
        "k": choose(),
        "x": cross_other(),
        "X": cross_own(),
        "p": project(),
    }
    order = "".join(ORDER)
    for n, letter in enumerate(order):
        if n == 2:
            for copy in local:
                copy.start()
        next(run[letter])
    for stages in run.values():
        assert next(stages, 0) == 0

    def score(k, carry):
        grad = all_grad[lists[s, k]].astype(F32)
        at = pl.ds(pl.multiple_of(LQ * k, LQ), LQ)
        folded = proj[at, :128] * grad[:, :128]
        for n in range(1, GB // 128):
            cols = slice(128 * n, 128 * n + 128)
            folded += proj[at, cols] * grad[:, cols]
        part[e, pl.ds(k, 1), :] = jnp.sum(folded, axis=0, keepdims=True)
        return carry

    lax.fori_loop(0, KQ, score, 0)

    parts_in = [
        remote(part.at[e], part.at[e], ps.at[d], pr.at[d], on_eig(d))
        for d in range(1, 8)
    ]
    for copy in parts_in:
        copy.wait_recv()
    full = part[0]
    for block in range(1, 8):
        full += part[block]
    full = jnp.concatenate([full, jnp.zeros((128 - KQ, 128), F32)], axis=0)
    out[...] = (jnp.sum(full.T, axis=0, keepdims=True) * FACTOR)[:, :KQ]

    for copy in sent:
        copy.wait_send()


def shards(
    cand_act, cand_grad, query_act, query_grad, act_basis, grad_basis, eigvals, query_lists,
    valid_len,
):
    anywhere = pl.BlockSpec(memory_space=pl.ANY)
    scalars = pl.BlockSpec(memory_space=pltpu.SMEM)
    dma = pltpu.SemaphoreType.DMA
    return pl.pallas_call(
        kernel,
        out_shape=jax.ShapeDtypeStruct((1, KQ), F32),
        in_specs=[scalars, scalars] + [anywhere] * 7,
        out_specs=pl.BlockSpec(memory_space=pltpu.VMEM),
        scratch_shapes=[
            pltpu.VMEM((DW, QUARTER), BF),
            pltpu.VMEM((640, DW), BF),
            pltpu.VMEM((640, QUARTER), F32),
            pltpu.VMEM((2, LEN, HALF), BF),
            pltpu.VMEM((8, 128, GB), BF),
            pltpu.VMEM((GB, LEN), BF),
            pltpu.VMEM((GB, GB), BF),
            pltpu.VMEM((GB, DW), F32),
            pltpu.VMEM((2, GB, HALF), BF),
            pltpu.VMEM((64, LQ, GB), BF),
            pltpu.VMEM((64, LQ, QUARTER), BF),
            pltpu.VMEM((2, KQ * LQ, HALF), BF),
            pltpu.VMEM((KQ * LQ, GB), F32),
            pltpu.VMEM((GB, HALF), F32),
            pltpu.VMEM((4, LQ, GB), BF),
            pltpu.VMEM((8, KQ, 128), F32),
            dma((10,)),
            dma((20,)), dma((20,)),
            dma((8,)), dma((8,)),
            dma((3,)), dma((3,)),
            dma((14,)), dma((14,)),
            dma((20,)), dma((20,)),
            dma((20,)), dma((20,)),
            dma((5,)), dma((5,)),
            dma((8,)), dma((8,)),
        ],
        compiler_params=pltpu.CompilerParams(
            collective_id=0, has_side_effects=True, vmem_limit_bytes=63 * 2**20
        ),
        name="influence",
    )(
        query_lists, valid_len, cand_act, cand_grad, query_act, query_grad, act_basis,
        grad_basis, eigvals,
    )


def solution(mesh):
    placed = (
        P("seq", "eig", None),
        P("seq", "eig", None),
        P("seq", None, None),
        P("seq", None, "eig"),
        P("seq", None),
        P("eig", None, None),
        P("eig", None),
        P(),
        P("seq"),
    )
    return jax.shard_map(
        shards, mesh=mesh, in_specs=placed, out_specs=P("seq", None), check_vma=False
    )
```

```python
import functools
import math

import jax
import jax.numpy as jnp
from jax import lax
from jax.experimental import pallas as pl
from jax.experimental.pallas import tpu as pltpu
from jax.sharding import PartitionSpec as P

DW = 2560
FW = 10240
LEN = 1024
LQ = 32
KQ = 16
GB = 1280
HALF = 1280
QUARTER = 640
BF = jnp.bfloat16
F32 = jnp.float32
MESH = pl.DeviceIdType.MESH
FACTOR = 1.0 / math.sqrt(FW * DW * LEN * LQ)
ORDER = (
    "brGwbbbbirGbbbib",
    "gMsigissasssatagtssgskggta",
    "XgaxaxgakXkpkpg",
)
LANES = (0, -1, 1, 2)


def wrap(i):
    return lax.rem(i + 8, 4)


def mm(a, b, dims=((1,), (0,))):
    return lax.dot_general(a, b, (dims, ((), ())), preferred_element_type=F32)


def kernel(
    lists, lens, cand_act, cand_grad, query_act, query_grad, act_basis, grad_basis, eigvals,
    out,
    basis, rows, total, act, grads, rot_t, gbasis, recip, scaled, all_grad, slim, chosen, proj, begun,
    raw_grad, part,
    loc, bs, br, gs, gr, cs, cr, as_, ar, qs, qr, hs, hr, ts, tr, ps, pr,
):
    s = lax.axis_index("seq")
    e = lax.axis_index("eig")
    z, x = lax.div(s, 4), lax.rem(s, 4)
    y, h = lax.div(e, 2), lax.rem(e, 2)
    parity = lax.rem(y, 2)
    other = 1 - parity
    lower = 1 - lax.rem(y + h, 2)

    def slot(da, db):
        return 4 * wrap(z + h * da + (1 - h) * db) + wrap(x + (1 - h) * da + h * db)

    def on_seq(da, db):
        return {"seq": slot(da, db), "eig": e}

    def on_y(d):
        return {"seq": s, "eig": 2 * wrap(y + d) + h}

    def on_eig(d):
        return {"seq": s, "eig": lax.rem(e + d, 8)}

    sibling = {"seq": s, "eig": 2 * y + 1 - h}

    def remote(src, dst, send, recv, device):
        copy = pltpu.make_async_remote_copy(
            src_ref=src, dst_ref=dst, send_sem=send, recv_sem=recv,
            device_id=device, device_id_type=MESH,
        )
        copy.start()
        sent.append(copy)
        return copy

    sent = []

    def at_rows(i):
        return pl.ds(pl.multiple_of(128 * i, 128), 128)

    quarter = pl.ds(pl.multiple_of(parity * HALF + h * QUARTER, 128), QUARTER)
    block_rows = pl.ds(pl.multiple_of(160 * s, 32), 160)
    place = 2 * wrap(y - 1 + lower) + 1 - lower
    local = [
        pltpu.make_async_copy(act_basis.at[:, quarter], basis.at[block_rows], loc.at[0]),
        pltpu.make_async_copy(query_grad, raw_grad, loc.at[1]),
        pltpu.make_async_copy(grad_basis.at[0], gbasis, loc.at[2]),
        pltpu.make_async_copy(cand_act.at[0], rows.at[at_rows(1 + lower)], loc.at[3]),
        pltpu.make_async_copy(
            cand_grad.at[0, :, pl.ds(pl.multiple_of(e * GB, 128), GB)], grads.at[place], loc.at[4]
        ),
        pltpu.make_async_copy(eigvals, recip, loc.at[5]),
    ]
    local += [
        pltpu.make_async_copy(query_act.at[n], rows.at[pl.ds(512 + LQ * n, LQ)], loc.at[6 + n])
        for n in range(4)
    ]

    barrier = pltpu.get_barrier_semaphore()
    greeted = [on_seq(1, 0), on_seq(-1, 0), on_seq(0, 1), on_seq(0, -1)]
    greeted += [on_eig(d) for d in range(1, 8)]
    for device in greeted:
        pl.semaphore_signal(barrier, inc=1, device_id=device, device_id_type=MESH)
    pl.semaphore_wait(barrier, len(greeted))

    def torus(view_of, own_of, send, recv, width=QUARTER):
        cols = pl.ds(0, width)
        view = functools.partial(view_of, cols)
        own = own_of(cols)

        def ship(n, src, where, part, device):
            return remote(src, view(where, part), send.at[n], recv.at[n], device)

        ring = {}
        ring[0] = ship(0, own, s, None, on_seq(1, 0))
        ring[1] = ship(1, own, s, None, on_seq(-1, 0))
        for side, db in ((0, 1), (1, -1)):
            ring[4 + side] = ship(4 + side, own, s, None, on_seq(0, db))
        yield

        def second(lane):
            da = LANES[lane]
            where = slot(da, 0)
            for side, db in ((0, 1), (1, -1)):
                n = 4 + 4 * lane + side
                ring[n] = ship(n, view(where, None), where, None, on_seq(0, db))

        def onward(lane):
            da = LANES[lane]
            for side, db in ((0, 1), (1, -1)):
                ring[4 + 4 * lane + side].wait_recv()
                where = slot(da, -db)
                n = 6 + 4 * lane + side
                ring[n] = ship(n, view(where, side), where, side, on_seq(0, db))

        for side, da in ((0, 1), (1, -1)):
            ring[side].wait_recv()
            where = slot(-da, 0)
            ring[2 + side] = ship(2 + side, view(where, side), where, side, on_seq(da, 0))
            second(1 + side)
            yield
        ring[2].wait_recv()
        ring[3].wait_recv()
        second(3)
        yield
        for lane in range(4):
            onward(lane)
            yield
        for lane in range(4):
            ring[6 + 4 * lane].wait_recv()
            ring[7 + 4 * lane].wait_recv()
        yield

    def basis_view(cols, where, part):
        if part is None:
            return basis.at[pl.ds(pl.multiple_of(160 * where, 32), 160), cols]
        return basis.at[pl.ds(pl.multiple_of(160 * where + 80 * part, 16), 80), cols]

    def own_basis(cols):
        first = parity * HALF + h * QUARTER + cols.start
        return act_basis.at[:, pl.ds(pl.multiple_of(first, 128), cols.size)]

    partner = {"seq": s, "eig": 2 * wrap(y + 2 * lower - 1) + h}

    def share_rows():
        near = rows.at[at_rows(1 + lower)]
        far = rows.at[at_rows(3 * lower)]
        first = remote(
            cand_act.at[0], rows.at[at_rows(3 * (1 - lower))], cs.at[0], cr.at[0], partner
        )
        across = [remote(cand_act.at[0], near, cs.at[1], cr.at[1], sibling)]
        yield
        first.wait_recv()
        across.append(remote(far, far, cs.at[2], cr.at[2], sibling))
        yield
        local[3].wait()
        for copy in across:
            copy.wait_recv()
        yield

    def share_grads():
        grads_in = []
        for offsets in ((2, 6), (3, 5, 4, 1, 7)):
            for d in offsets:
                to = lax.rem(e + d, 8)
                cols = pl.ds(pl.multiple_of(to * GB, 128), GB)
                copy = remote(
                    cand_grad.at[0, :, cols], grads.at[place], gs.at[d], gr.at[d], on_eig(d)
                )
                grads_in.append(copy)
            yield
        local[4].wait()
        for copy in grads_in:
            copy.wait_recv()
        yield

    def rotate_grads():
        next(run["G"])

        def turn(i, carry):
            cols = pl.ds(pl.multiple_of(i * 256, 256), 256)
            turned = mm(grads[...].reshape(LEN, GB), gbasis[:, cols]).astype(BF)
            rot_t[cols, :] = turned.T
            return carry

        for first, last in ((0, 2), (2, 4), (4, 5)):
            lax.fori_loop(first, last, turn, 0)
            yield

    def own_grads():
        local[1].wait()
        local[2].wait()

        def turn(i, carry):
            cols = pl.ds(pl.multiple_of(i * 256, 256), 256)
            turned = mm(raw_grad[...].reshape(128, GB), gbasis[:, cols]).astype(BF)
            all_grad[pl.ds(4 * s, 4), :, cols] = turned.reshape(4, LQ, 256)
            return carry

        lax.fori_loop(0, 5, turn, 0)
        yield

    def grad_view(cols, where, part):
        if part is None:
            return all_grad.at[pl.ds(4 * where, 4), :, cols]
        return all_grad.at[pl.ds(4 * where + 2 * part, 2), :, cols]

    def invert():
        local[5].wait()

        def body(i, carry):
            at = pl.ds(pl.multiple_of(i * 64, 64), 64)
            recip[at, :] = 1.0 / recip[at, :]
            return carry

        for first in range(0, 20, 5):
            lax.fori_loop(first, first + 5, body, 0)
            yield

    mine = pl.ds(pl.multiple_of(h * QUARTER, 128), QUARTER)

    def rotate_rows():
        local[0].wait()
        for copy in local[6:]:
            copy.wait()
        next(run["r"])

        def add(i, carry):
            at = pl.ds(pl.multiple_of(i * 512, 512), 512)
            total[...] += mm(rows[:, at], basis[at, :])
            return carry

        total[...] = jnp.zeros_like(total)
        lax.fori_loop(0, 5, add, 0)
        length = lens[0]
        r = lax.broadcasted_iota(jnp.int32, (128, 1), 0)
        for n, (chip, core) in enumerate(((-1, other), (0, other), (0, parity), (1, parity))):
            token = 256 * wrap(y + chip) + 128 * core + r
            turned = total[128 * n : 128 * n + 128].astype(BF)
            at = pl.ds(pl.multiple_of(256 * wrap(y - 1 + n // 2) + 128 * (n % 2), 128), 128)
            act[parity, at, mine] = jnp.where(token < length, turned, jnp.zeros((), BF))
        slim[pl.ds(4 * s, 4)] = total[512:640].astype(BF).reshape(4, LQ, QUARTER)
        yield

    def act_view(half, block):
        return act.at[half, pl.ds(pl.multiple_of(256 * block, 256), 256), mine]

    def gather_act():
        def ship(n, half, block, device):
            view = act_view(half, block)
            return remote(view, view, as_.at[n], ar.at[n], device)

        ring = {}
        for side, d in ((0, 1), (1, -1)):
            ring[side] = ship(side, parity, wrap(y - 1 + side), on_y(d))
        for side, d in ((0, 1), (1, -1)):
            ring[2 + side] = ship(2 + side, parity, wrap(y - side), on_y(d))
        across = [ship(6 + side, parity, wrap(y - 1 + side), sibling) for side in (0, 1)]
        yield
        for copy in across[:2]:
            copy.wait_recv()
        yield
        for side, d in ((0, 1), (1, -1)):
            ring[side].wait_recv()
            block = wrap(y - d - 1 + side)
            ring[4 + side] = ship(4 + side, other, block, on_y(d))
            across.append(ship(8 + side, other, block, sibling))
        yield
        for side, d in ((0, 1), (1, -1)):
            ring[2 + side].wait_recv()
            across.append(ship(10 + side, other, wrap(y - d - side), sibling))
        yield
        for copy in across[2:6]:
            copy.wait_recv()
        yield
        for side in (0, 1):
            ring[4 + side].wait_recv()
            across.append(ship(12 + side, parity, wrap(y + 1 + side), sibling))
        yield
        for copy in across[6:]:
            copy.wait_recv()
        yield

    def slim_view(cols, where, part):
        if part is None:
            return slim.at[pl.ds(4 * where, 4), :, cols]
        return slim.at[pl.ds(4 * where + 2 * part, 2), :, cols]

    def choose():
        def ship(n, half, piece, device):
            view = chosen.at[half, :, mine]
            if piece is not None:
                view = chosen.at[half, pl.ds(256 * piece, 256), mine]
            return remote(view, view, ts.at[n], tr.at[n], device)

        for k in range(KQ):
            chosen[parity, LQ * k : LQ * k + LQ, mine] = slim[lists[s, k]]
        near = [ship(0, parity, 0, on_y(1)), ship(1, parity, 1, on_y(-1))]
        across = [ship(2, parity, None, sibling)]
        yield
        across[0].wait_recv()
        yield
        for side in (0, 1):
            near[side].wait_recv()
            across.append(ship(3 + side, other, side, sibling))
        yield
        for copy in across[1:]:
            copy.wait_recv()
        yield

    def cross_other():
        def body(i, carry):
            cols = pl.ds(pl.multiple_of(i * 256, 256), 256)
            wide = pl.ds(pl.multiple_of(other * HALF + i * 256, 256), 256)
            block = mm(rot_t[...], act[other, :, cols])
            scaled[other, :, cols] = (block * recip[:, wide]).astype(BF)
            return carry

        for first, last in ((0, 2), (2, 5)):
            lax.fori_loop(first, last, body, 0)
            yield

    def cross_own():
        def two(block, cols):
            at = [pl.ds(pl.multiple_of(256 * wrap(block + n), 256), 256) for n in (0, 1)]
            return mm(rot_t[:, at[0]], act[parity, at[0], cols]) + mm(
                rot_t[:, at[1]], act[parity, at[1], cols]
            )

        def begin(i, carry):
            cols = pl.ds(pl.multiple_of(i * 256, 256), 256)
            begun[:, cols] = two(y - 1, cols)
            return carry

        def finish(i, carry):
            cols = pl.ds(pl.multiple_of(i * 256, 256), 256)
            wide = pl.ds(pl.multiple_of(parity * HALF + i * 256, 256), 256)
            block = begun[:, cols] + two(y + 1, cols)
            scaled[parity, :, cols] = (block * recip[:, wide]).astype(BF)
            return carry

        lax.fori_loop(0, 5, begin, 0)
        yield
        lax.fori_loop(0, 5, finish, 0)
        yield

    def project():
        proj[...] = mm(chosen[parity], scaled[parity], ((1,), (1,)))
        yield
        proj[...] += mm(chosen[other], scaled[other], ((1,), (1,)))
        yield

    run = {
        "b": torus(basis_view, own_basis, bs, br),
        "r": share_rows(),
        "G": share_grads(),
        "w": own_grads(),
        "g": torus(grad_view, lambda cols: grad_view(cols, s, None), hs, hr, GB),
        "s": torus(slim_view, lambda cols: slim_view(cols, s, None), qs, qr),
        "i": invert(),
        "M": rotate_rows(),
        "a": gather_act(),
        "t": rotate_grads(),
        "k": choose(),
        "x": cross_other(),
        "X": cross_own(),
        "p": project(),
    }
    order = "".join(ORDER)
    for n, letter in enumerate(order):
        if n == 2:
            for copy in local:
                copy.start()
        next(run[letter])
    for stages in run.values():
        assert next(stages, 0) == 0

    def score(k, carry):
        grad = all_grad[lists[s, k]].astype(F32)
        at = pl.ds(pl.multiple_of(LQ * k, LQ), LQ)
        folded = proj[at, :128] * grad[:, :128]
        for n in range(1, GB // 128):
            cols = slice(128 * n, 128 * n + 128)
            folded += proj[at, cols] * grad[:, cols]
        part[e, pl.ds(k, 1), :] = jnp.sum(folded, axis=0, keepdims=True)
        return carry

    lax.fori_loop(0, KQ, score, 0)

    parts_in = [
        remote(part.at[e], part.at[e], ps.at[d], pr.at[d], on_eig(d))
        for d in range(1, 8)
    ]
    for copy in sent:
        copy.wait_send()
    for copy in parts_in:
        copy.wait_recv()
    full = part[0]
    for block in range(1, 8):
        full += part[block]
    full = jnp.concatenate([full, jnp.zeros((128 - KQ, 128), F32)], axis=0)
    out[...] = (jnp.sum(full.T, axis=0, keepdims=True) * FACTOR)[:, :KQ]


def shards(
    cand_act, cand_grad, query_act, query_grad, act_basis, grad_basis, eigvals, query_lists,
    valid_len,
):
    anywhere = pl.BlockSpec(memory_space=pl.ANY)
    scalars = pl.BlockSpec(memory_space=pltpu.SMEM)
    dma = pltpu.SemaphoreType.DMA
    return pl.pallas_call(
        kernel,
        out_shape=jax.ShapeDtypeStruct((1, KQ), F32),
        in_specs=[scalars, scalars] + [anywhere] * 7,
        out_specs=pl.BlockSpec(memory_space=pltpu.VMEM),
        scratch_shapes=[
            pltpu.VMEM((DW, QUARTER), BF),
            pltpu.VMEM((640, DW), BF),
            pltpu.VMEM((640, QUARTER), F32),
            pltpu.VMEM((2, LEN, HALF), BF),
            pltpu.VMEM((8, 128, GB), BF),
            pltpu.VMEM((GB, LEN), BF),
            pltpu.VMEM((GB, GB), BF),
            pltpu.VMEM((GB, DW), F32),
            pltpu.VMEM((2, GB, HALF), BF),
            pltpu.VMEM((64, LQ, GB), BF),
            pltpu.VMEM((64, LQ, QUARTER), BF),
            pltpu.VMEM((2, KQ * LQ, HALF), BF),
            pltpu.VMEM((KQ * LQ, GB), F32),
            pltpu.VMEM((GB, HALF), F32),
            pltpu.VMEM((4, LQ, GB), BF),
            pltpu.VMEM((8, KQ, 128), F32),
            dma((10,)),
            dma((20,)), dma((20,)),
            dma((8,)), dma((8,)),
            dma((3,)), dma((3,)),
            dma((14,)), dma((14,)),
            dma((20,)), dma((20,)),
            dma((20,)), dma((20,)),
            dma((5,)), dma((5,)),
            dma((8,)), dma((8,)),
        ],
        compiler_params=pltpu.CompilerParams(
            collective_id=0, has_side_effects=True, vmem_limit_bytes=63 * 2**20
        ),
        name="influence",
    )(
        query_lists, valid_len, cand_act, cand_grad, query_act, query_grad, act_basis,
        grad_basis, eigvals,
    )


def solution(mesh):
    placed = (
        P("seq", "eig", None),
        P("seq", "eig", None),
        P("seq", None, None),
        P("seq", None, "eig"),
        P("seq", None),
        P("eig", None, None),
        P("eig", None),
        P(),
        P("seq"),
    )
    return jax.shard_map(
        shards, mesh=mesh, in_specs=placed, out_specs=P("seq", None), check_vma=False
    )
```
